512 devices in a mesh: expert: 64 (over x, z, core), group: 8 (over y).
Axes of the slice: x: 4, y: 8, z: 8, core: 2. Of those that a mesh axis runs over, the one named last changes fastest.
Arguments:
- tokens: bfloat16 [32768, 2048], P(('expert', 'group')), may hold values from -6 to 6
- expert_ids: int32 [32768, 2], P(('expert', 'group')), may hold values from 0 to 63, all different within a row; in each aligned block of 64 rows (0 to 63, 64 to 127, ...) at most 2 rows name the same one
- gates: float32 [32768, 2], P(('expert', 'group')), may hold values from 0.2 to 1
- ln_gain: float32 [2048], replicated, may hold values from 0.25 to 2.5
- w_in: bfloat16 [64, 2048, 4096], P('expert', None, 'group'), may hold values from -0.125 to 0.125
- b_in: float32 [64, 4096], P('expert', 'group'), may hold values from -3 to 3
- w_out: bfloat16 [64, 4096, 2048], P('expert', 'group'), may hold values from -0.125 to 0.125
- b_out: float32 [64, 2048], P('expert'), may hold values from -3 to 3
- final_gain: float32 [2048], replicated, may hold values from 0.1 to 1.9
- w_cross: bfloat16 [2048, 2048], P('expert', 'group'), may hold values from -0.125 to 0.125
- lengths: int32 [512, 4], replicated, may hold values from 1 to 32, 64 in all within a row
- page_table: int32 [512, 4], replicated, may hold values from 0 to 63, as said below
- queries: bfloat16 [2048, 1024], P('expert', 'group'), may hold values from -25 to 25
Outputs:
- encoded: bfloat16 [32768, 2048], P(('expert', 'group'))
- context: bfloat16 [2048, 1024], P('expert', 'group')
The draws below stay inside these ranges and needn't reach their ends.
Inputs may be any that keep to these rules, and one draw needn't show every extreme that they name: `expert_ids`: in the 64 rows of one device every expert is named exactly 2 times; a row names two different experts. `lengths`: every row sums to 64. For each group index g and sentence number k there is a shift s with page_table[c * 8 + g, k] = (c + s) mod 64 for every c; the shifts of the 32 pairs (g, k) are distinct.
All inputs are finite; a program needn't handle non-finite values.
Results may differ from the reference program's by a relative error of at most 0.04.
Values may be sent and summed in bfloat16 or wider, within the bound.
No kernel may reach another device: no remote copies, remote signals or barrier semaphores. Data moves between devices by JAX's collectives and lax.ppermute only.
A program may use at most 64 MiB of HBM per device.

```python
import math
import jax
import jax.numpy as jnp
import numpy as np
from jax import lax

D = 2048
FF_WIN = 4096
HS = 128
TOK_DEV = 64
SENT_DEV = 4
EXPERTS = 64
HEADS = 8
FF_DEV = 512
CAP = 2
MAXLEN = 32
TOKENS = 32768
SENTS = 2048
N_EXPERT = 64
N_GROUP = 8


def draw_page_table(key, part):
    key = jax.random.fold_in(key, 11)
    values = jax.random.permutation(key, N_EXPERT).astype(jnp.int32)
    index = jnp.arange(N_EXPERT, dtype=jnp.int32)
    priority = jnp.where(values == 1, -2, jnp.where(values == N_EXPERT // 2, -1, index)).astype(jnp.int32)
    order = values[jnp.argsort(priority, stable=True)]
    mixing = jax.random.permutation(jax.random.fold_in(key, 5), N_GROUP * SENT_DEV).astype(jnp.int32)
    shifts = order[:N_GROUP * SENT_DEV][mixing].reshape(N_GROUP, SENT_DEV)
    column = jnp.arange(N_EXPERT, dtype=jnp.int32)
    table = (column[:, None, None] + shifts[None, :, :]) % N_EXPERT
    return table.reshape(N_EXPERT * N_GROUP, SENT_DEV).astype(jnp.int32)


def draw_queries(key, part):
    key = jax.random.fold_in(key, 23)
    first_key = jax.random.fold_in(key, 0)
    values = jnp.clip(jax.random.normal(first_key, (SENTS, HEADS * HS), jnp.float32), -6.0, 6.0)
    return values.astype(jnp.bfloat16)


def level_of(own_key, extent, pieces, least, top_value):
    factor_of = 1.0
    for axis_at, parts in pieces:
        heights = jax.random.uniform(jax.random.fold_in(jax.random.fold_in(own_key, 6), axis_at), (parts,), jnp.float32, least / len(pieces), top_value / len(pieces))
        factor_of = factor_of * jnp.repeat(jnp.exp(heights), extent[axis_at] // parts).reshape((-1,) + (1,) * (len(extent) - 1 - axis_at))
    return factor_of


def length_profile(amount, total, limit, lean):
    loads = [(1 << 20) // math.isqrt(rank ** lean) + 1 for rank in range(2, amount + 1)]
    rest, holding = total - limit - (amount - 1), [1] * (amount - 1)
    while rest > 0:
        free = [i for i in range(amount - 1) if holding[i] < limit]
        pool, budget = sum([loads[i] for i in free]), rest
        for i in free:
            more = min(limit - holding[i], max(1, budget * loads[i] // pool), rest)
            holding[i] = holding[i] + more
            rest = rest - more
    return np.array([limit] + holding)


def uneven(stream_key, number_of, total, most, lean):
    if number_of == 2:
        one = jax.random.randint(stream_key, (), max(1, total - most), min(most, total - 1) + 1)
        return jnp.stack([one, total - one])
    tallies = jnp.asarray(length_profile(number_of, total, most, lean), jnp.int32)
    couples = (number_of - 1) // 2
    source_of, sink = tallies[1:1 + 2 * couples:2], tallies[2:2 + 2 * couples:2]
    margin = jnp.minimum(source_of - 1, most - sink)
    moved = jax.random.randint(jax.random.fold_in(stream_key, 1), (couples,), 0, 1 << 20) % (margin + 1)
    tallies = tallies.at[1:1 + 2 * couples:2].set(source_of - moved).at[2:2 + 2 * couples:2].set(sink + moved)
    return tallies[jax.random.permutation(jax.random.fold_in(stream_key, 2), number_of)]


def deal_out(own_key, own, number, rows, count, top, limit, skew):
    ranking = jax.random.permutation(own_key, count)
    packed, ordinary = load_shares(count, rows * top, limit, skew, True), load_shares(count, rows * top, limit, skew, False)
    places = jnp.arange(count)

    def named(tallies, turn):
        used = int((tallies > 0).sum())
        fixed = max(1, used // 4)
        passed = fixed + (places - fixed + turn * (used - fixed)) % max(1, count - fixed)
        return jnp.zeros((count,), jnp.int32).at[ranking[jnp.where(places < fixed, places, passed)]].set(jnp.asarray(tallies, jnp.int32))

    tallies = jnp.where(number % 4 == 0, named(packed, number // 4), named(ordinary, number - number // 4 - 1))
    mixed = jax.random.permutation(jax.random.fold_in(own, 3), count)
    giver, sink = mixed[0:count // 2 * 2:2], mixed[1:count // 2 * 2:2]
    slack = jnp.minimum(tallies[giver] - 1, limit - tallies[sink]) // 2
    slack = jnp.where((giver == ranking[0]) | (sink == ranking[0]) | (tallies[sink] == 0), 0, jnp.maximum(slack, 0))
    passed = jax.random.randint(jax.random.fold_in(own, 4), (count // 2,), 0, 1 << 20) % (slack + 1)
    tallies = tallies.at[giver].add(-passed).at[sink].add(passed)
    members = jnp.searchsorted(jnp.cumsum(tallies), jnp.arange(rows * top), side="right").astype(jnp.int32)
    table = members.reshape(top, rows).T
    table = table[jax.random.permutation(jax.random.fold_in(own, 1), rows)]
    turn = jax.random.randint(jax.random.fold_in(own, 2), (rows, 1), 0, top)
    return jnp.take_along_axis(table, (jnp.arange(top)[None, :] + turn) % top, axis=1)


def load_shares(count, total, limit, lean, full):
    portions = [(1 << 20) // math.isqrt(rank ** lean) + 1 for rank in range(1, count + 1)]
    largest = limit if full else min(limit, max(-(-total // count), total * portions[0] // sum(portions)))
    least = 1 if total - largest >= count - 1 else 0
    holding, spare = [largest] + [least] * (count - 1), total - largest - least * (count - 1)
    while spare > 0:
        free = [i for i in range(1, count) if holding[i] < largest] or [i for i in range(1, count) if holding[i] < limit]
        mass, remaining = sum([portions[i] for i in free]), spare
        for i in free:
            extra = min(limit - holding[i], max(1, remaining * portions[i] // mass), spare)
            holding[i] = holding[i] + extra
            spare = spare - extra
    return np.array(holding)


def gaussian(rng, extent, width, limit, pieces=(), held_as=jnp.bfloat16):
    values = width * jax.random.normal(rng, extent, jnp.float32)
    if pieces:
        values = values * level_of(rng, extent, pieces, -0.22, 0.18)
    return jnp.clip(values, -limit, limit).astype(held_as)


def setup_inputs(seed: int = 0) -> dict:
    splits = jax.random.split(jax.random.key(seed), 14)
    tokens = gaussian(splits[0], (TOKENS, D), 1.0, 6.0, ((0, 512),))
    expert_ids_keys = jax.random.split(jax.random.fold_in(splits[1], 1), TOKENS // TOK_DEV)
    expert_ids_turns = jax.random.permutation(jax.random.fold_in(splits[1], 3), TOKENS // TOK_DEV)
    expert_ids = jax.vmap(lambda own, number: deal_out(jax.random.fold_in(splits[1], 2), own, number, TOK_DEV, EXPERTS, 2, CAP, 1))(expert_ids_keys, expert_ids_turns).reshape((TOKENS, 2))
    gates = jnp.clip(0.2 + 0.8 * jax.random.uniform(splits[2], (TOKENS, 2), jnp.float32) ** level_of(splits[2], (TOKENS, 2), ((0, 512),), -0.2, 0.2), 0.2, 1.0)
    ln_gain = jnp.clip(jnp.exp(jax.random.uniform(splits[3], (D,), jnp.float32, math.log(0.25), math.log(2.5))), 0.25, 2.5)
    w_in = gaussian(splits[4], (EXPERTS, D, FF_WIN), D ** -0.5, 0.125, ((0, 64), (2, 8)))
    b_in = gaussian(splits[5], (EXPERTS, FF_WIN), 0.5, 3.0, ((0, 64), (1, 8)), jnp.float32)
    w_out = gaussian(splits[6], (EXPERTS, FF_WIN, D), (FF_WIN // 2) ** -0.5, 0.125, ((0, 64), (1, 8)))
    b_out = gaussian(splits[7], (EXPERTS, D), 0.5, 3.0, ((0, 64),), jnp.float32)
    final_gain = jnp.clip(1.0 + 0.18 * jax.random.normal(splits[8], (D,), jnp.float32), 0.1, 1.9)
    w_cross = gaussian(splits[9], (D, HEADS * 2 * HS), D ** -0.5, 0.125, ((0, 64), (1, 8)))
    lengths = jax.vmap(lambda own: uneven(own, SENT_DEV, TOK_DEV, MAXLEN, 2))(jax.random.split(splits[10], (N_EXPERT * N_GROUP))).reshape((N_EXPERT * N_GROUP, SENT_DEV)).astype(jnp.int32)
    page_table = draw_page_table(jax.random.fold_in(splits[13], 71), 0)
    queries = draw_queries(jax.random.fold_in(splits[13], 71), 0)
    return {"tokens": tokens, "expert_ids": expert_ids, "gates": gates, "ln_gain": ln_gain, "w_in": w_in, "b_in": b_in, "w_out": w_out, "b_out": b_out, "final_gain": final_gain, "w_cross": w_cross, "lengths": lengths, "page_table": page_table, "queries": queries}


EPSILON = 1e-05

def layer_norm(values, gain_row):
    average = lax.optimization_barrier(jnp.mean(values, axis=-1, keepdims=True))
    centred = values - average
    variance = lax.optimization_barrier(jnp.mean(centred * centred, axis=-1, keepdims=True))
    return centred * lax.rsqrt(variance + EPSILON) * gain_row.astype(jnp.float32)

def slot_numbers(id_rows):
    flat_ids = id_rows.reshape(-1)
    count = flat_ids.shape[0]
    same_expert = (flat_ids[:, None] == flat_ids[None, :]).astype(jnp.int32)
    position = jnp.arange(count, dtype=jnp.int32)
    earlier = (position[None, :] < position[:, None]).astype(jnp.int32)
    return lax.optimization_barrier(jnp.sum(same_expert * earlier, axis=1)).astype(jnp.int32)

def reference(tokens, expert_ids, gates, ln_gain, w_in, b_in, w_out, b_out, final_gain, w_cross, lengths, page_table, queries):
    blocks = N_EXPERT * N_GROUP
    normed = layer_norm(tokens.astype(jnp.float32), ln_gain).astype(jnp.bfloat16)
    block_ids = expert_ids.reshape(blocks, 2 * TOK_DEV)
    slot_rank = jax.vmap(slot_numbers)(block_ids)
    block_index = jnp.arange(blocks, dtype=jnp.int32)[:, None]
    token_index = block_index * TOK_DEV + jnp.arange(2 * TOK_DEV, dtype=jnp.int32)[None, :] // 2
    position = block_index * CAP + slot_rank
    table = jnp.full((EXPERTS, blocks * CAP), TOKENS, jnp.int32).at[block_ids, position].set(token_index)
    gate_table = jnp.zeros((EXPERTS, blocks * CAP), jnp.float32).at[block_ids, position].set(gates.reshape(blocks, 2 * TOK_DEV))
    padded = jnp.concatenate([normed, jnp.zeros((1, D), jnp.bfloat16)], axis=0)

    def expert_step(running, inputs):
        row_index, row_gates, first, first_bias, second, second_bias = inputs
        routed = padded[row_index]
        hidden = jax.nn.relu(jnp.dot(routed, first, preferred_element_type=jnp.float32) + first_bias).astype(jnp.bfloat16)
        hidden_blocks = hidden.reshape(-1, N_GROUP, FF_DEV).astype(jnp.float32)
        second_blocks = second.reshape(N_GROUP, FF_DEV, D).astype(jnp.float32)
        partial_value = jnp.einsum('rgf,gfd->grd', hidden_blocks, second_blocks)
        rounded = lax.optimization_barrier(partial_value.astype(jnp.bfloat16))
        summed = lax.optimization_barrier(jnp.sum(rounded.astype(jnp.float32), axis=0))
        expert_out = (summed + second_bias).astype(jnp.bfloat16)
        running = running.at[row_index].add(row_gates[:, None] * expert_out.astype(jnp.float32))
        return (running, None)
    start = jnp.zeros((TOKENS + 1, D), jnp.float32)
    moe_total, _ = lax.scan(expert_step, start, (table, gate_table, w_in, b_in, w_out, b_out))
    moe = moe_total[:TOKENS]
    encoded = layer_norm(tokens.astype(jnp.float32) + moe, final_gain).astype(jnp.bfloat16)
    keyvals = jnp.dot(encoded, w_cross, preferred_element_type=jnp.float32).astype(jnp.bfloat16)
    starts = block_index * TOK_DEV + (jnp.cumsum(lengths, axis=1) - lengths).astype(jnp.int32)
    offsets = jnp.arange(MAXLEN, dtype=jnp.int32)
    row_index = jnp.minimum(starts[:, :, None] + offsets[None, None, :], TOKENS - 1)
    gathered = keyvals[row_index].reshape(blocks, SENT_DEV, MAXLEN, HEADS, 2, HS).astype(jnp.float32)
    key_part = gathered[:, :, :, :, 0, :]
    value_part = gathered[:, :, :, :, 1, :]
    sentence_number = jnp.arange(SENT_DEV, dtype=jnp.int32)[None, :]
    query_index = page_table * (N_GROUP * SENT_DEV) + block_index % N_GROUP * SENT_DEV + sentence_number
    query_rows = queries[query_index].reshape(blocks, SENT_DEV, HEADS, HS).astype(jnp.float32)
    scores = jnp.einsum('dkhs,dkrhs->dkhr', query_rows, key_part) / math.sqrt(HS)
    visible = offsets[None, None, None, :] < lengths[:, :, None, None]
    scores = jnp.where(visible, scores, -jnp.inf)
    highest = lax.optimization_barrier(jnp.max(scores, axis=-1, keepdims=True))
    exponent = jnp.exp(scores - highest)
    attention = (exponent / lax.optimization_barrier(jnp.sum(exponent, axis=-1, keepdims=True))).astype(jnp.bfloat16)
    context_rows = jnp.einsum('dkhr,dkrhs->dkhs', attention.astype(jnp.float32), value_part).astype(jnp.bfloat16)
    context = jnp.zeros((SENTS, HEADS * HS), jnp.bfloat16).at[query_index.reshape(-1)].set(context_rows.reshape(-1, HEADS * HS))
    return (encoded, context)
```

```python
import math

import jax
import jax.numpy as jnp
from jax import lax
from jax.sharding import PartitionSpec as P

EPSILON = 1e-05
BF = jnp.bfloat16
F32 = jnp.float32


def layer_norm(values, gain_row):
    average = jnp.mean(values, axis=-1, keepdims=True)
    centred = values - average
    variance = jnp.mean(centred * centred, axis=-1, keepdims=True)
    return centred * lax.rsqrt(variance + EPSILON) * gain_row


def slot_numbers(id_rows):
    flat_ids = id_rows.reshape(-1)
    count = flat_ids.shape[0]
    same_expert = (flat_ids[:, None] == flat_ids[None, :]).astype(jnp.int32)
    position = jnp.arange(count, dtype=jnp.int32)
    earlier = (position[None, :] < position[:, None]).astype(jnp.int32)
    return jnp.sum(same_expert * earlier, axis=1)


def dot(a, b):
    return jnp.dot(a, b, preferred_element_type=F32)


def shift(value, by, groups):
    return lax.ppermute(value, "group", [(i, (i + by) % groups) for i in range(groups)])


def ring_gather(chunks, groups):
    half = groups // 2
    blocks = {0: list(chunks)}
    forward, backward = list(chunks), list(chunks)
    for step in range(1, half):
        for c in range(2):
            forward[c] = shift(forward[c], 1, groups)
            backward[c] = shift(backward[c], -1, groups)
        blocks[-step] = list(forward)
        blocks[step] = list(backward)
    blocks[half] = [shift(forward[0], 1, groups), shift(backward[1], -1, groups)]
    return blocks


def ring_scatter(partial, groups):
    half = groups // 2
    totals = []
    lengths = [(half - 1, half), (half, half - 1)]
    running = [[None, None], [None, None]]
    for step in range(half):
        for c in range(2):
            for way, sign in ((0, 1), (1, -1)):
                hops = lengths[c][way]
                if step >= hops:
                    continue
                offset = sign * (hops - step)
                if offset == -half:
                    offset = half
                value = partial(offset, c)
                if running[c][way] is not None:
                    value = value + running[c][way].astype(F32)
                running[c][way] = shift(value.astype(BF), sign, groups)
    for c in range(2):
        totals.append(
            partial(0, c) + running[c][0].astype(F32) + running[c][1].astype(F32)
        )
    return totals


def on_device(
    tokens,
    expert_ids,
    gates,
    ln_gain,
    w_in,
    b_in,
    w_out,
    b_out,
    final_gain,
    w_cross,
    lengths,
    page_table,
    queries,
):
    rows_dev, width = tokens.shape
    experts = lax.axis_size("expert")
    groups = lax.axis_size("group")
    capacity = 2 * rows_dev // experts
    places = experts * capacity
    sentences = lengths.shape[1]
    head_size = queries.shape[1]
    column = lax.axis_index("expert")
    row = lax.axis_index("group")
    first, second = w_in[0], w_out[0]
    half_width = width // 2

    cross_cols = w_cross.shape[1]
    own_cross = jnp.concatenate([w_cross, queries], axis=1)
    cross_rows = lax.all_gather(own_cross, "group", axis=0, tiled=False)
    cross_rows = jnp.concatenate(
        [
            cross_rows[:, :, :cross_cols].transpose(1, 0, 2).reshape(own_cross.shape[0], -1),
            cross_rows[:, :, cross_cols:].transpose(1, 0, 2).reshape(own_cross.shape[0], -1),
        ],
        axis=1,
    )
    cross = lax.all_gather(cross_rows, "expert", axis=0, tiled=True)
    cross_weights = cross[:, : groups * cross_cols]

    normed = layer_norm(tokens.astype(F32), ln_gain).astype(BF)
    target = (expert_ids.reshape(-1) * capacity + slot_numbers(expert_ids)).reshape(rows_dev, 2)
    place_ids = jnp.arange(places, dtype=jnp.int32)
    goes = (
        (place_ids[:, None] == target[None, :, 0]) | (place_ids[:, None] == target[None, :, 1])
    ).astype(BF)
    outgoing = dot(goes, normed).astype(BF).reshape(experts, capacity, width)
    arrived = lax.all_to_all(outgoing, "expert", 0, 0, tiled=True).reshape(places, width)

    blocks = ring_gather([arrived[:, :half_width], arrived[:, half_width:]], groups)
    hidden = {}
    for offset, halves in blocks.items():
        value = dot(halves[0], first[:half_width]) + dot(halves[1], first[half_width:])
        hidden[offset] = jax.nn.relu(value + b_in[0]).astype(BF)

    def partial(offset, c):
        return dot(hidden[offset], second[:, c * half_width : (c + 1) * half_width])

    sums = jnp.concatenate(ring_scatter(partial, groups), axis=1)
    expert_out = (sums + b_out[0]).astype(BF).reshape(experts, capacity, width)
    returned = lax.all_to_all(expert_out, "expert", 0, 0, tiled=True).reshape(places, width)

    moe = 0.0
    for k in range(2):
        picks = (target[:, k][:, None] == place_ids[None, :]).astype(BF)
        moe = moe + gates[:, k][:, None] * dot(picks, returned)
    encoded = layer_norm(tokens.astype(F32) + moe, final_gain).astype(BF)

    keyvals = dot(encoded, cross_weights).astype(BF).reshape(rows_dev, groups, 2, head_size)
    block = column * groups + row
    own_lengths = lax.dynamic_slice_in_dim(lengths, block, 1, 0)[0]
    owners = lax.dynamic_slice_in_dim(page_table, block, 1, 0)[0]
    slots_dev = groups * sentences
    own_queries = jnp.concatenate(
        [
            lax.dynamic_slice(
                cross,
                (owners[k] * slots_dev + row * sentences + k, groups * cross_cols),
                (1, groups * head_size),
            )
            for k in range(sentences)
        ],
        axis=0,
    ).reshape(sentences, groups, head_size)
    scores = jnp.einsum(
        "khs,rhs->hkr", own_queries, keyvals[:, :, 0], preferred_element_type=F32
    ) / math.sqrt(head_size)
    ends = jnp.cumsum(own_lengths)
    starts = ends - own_lengths
    row_ids = jnp.arange(rows_dev, dtype=jnp.int32)
    visible = (row_ids[None, :] >= starts[:, None]) & (row_ids[None, :] < ends[:, None])
    scores = jnp.where(visible[None], scores, -jnp.inf)
    highest = jnp.max(scores, axis=-1, keepdims=True)
    exponent = jnp.exp(scores - highest)
    attention = (exponent / jnp.sum(exponent, axis=-1, keepdims=True)).astype(BF)
    own_context = jnp.einsum(
        "hkr,rhs->hks", attention, keyvals[:, :, 1], preferred_element_type=F32
    ).astype(BF)

    slots = lax.all_to_all(own_context, "group", 0, 0, tiled=True).reshape(slots_dev, head_size)
    column_ids = jnp.arange(experts, dtype=jnp.int32)
    column_owners = lax.dynamic_slice_in_dim(page_table, column * groups, groups, 0).reshape(-1)
    to_owner = (column_ids[:, None] == column_owners[None, :]).astype(BF)
    sent = dot(to_owner, slots).astype(BF).reshape(experts, 1, head_size)
    received = lax.all_to_all(sent, "expert", 0, 0, tiled=True).reshape(experts, head_size)
    first_owners = page_table[:groups].reshape(-1)
    source = lax.rem(column - first_owners + experts, experts)
    from_source = (source[:, None] == column_ids[None, :]).astype(BF)
    context = dot(from_source, received).astype(BF)
    return (encoded, context)


def solution(mesh):
    return jax.shard_map(
        on_device,
        mesh=mesh,
        in_specs=(
            P(("expert", "group"), None),
            P(("expert", "group"), None),
            P(("expert", "group"), None),
            P(),
            P("expert", None, "group"),
            P("expert", "group"),
            P("expert", "group", None),
            P("expert", None),
            P(),
            P("expert", "group"),
            P(),
            P(),
            P("expert", "group"),
        ),
        out_specs=(P(("expert", "group"), None), P("expert", "group")),
        check_vma=False,
    )
```

```python
import math

import jax
import jax.numpy as jnp
from jax import lax
from jax.experimental import pallas as pl
from jax.experimental.pallas import tpu as pltpu
from jax.sharding import PartitionSpec as P

EPSILON = 1e-05
PAD_ROWS = 192
BF = jnp.bfloat16
F32 = jnp.float32


def layer_norm(values, gain_row):
    average = jnp.mean(values, axis=-1, keepdims=True)
    centred = values - average
    variance = jnp.mean(centred * centred, axis=-1, keepdims=True)
    return centred * lax.rsqrt(variance + EPSILON) * gain_row


def slot_numbers(id_rows):
    flat_ids = id_rows.reshape(-1)
    count = flat_ids.shape[0]
    same_expert = (flat_ids[:, None] == flat_ids[None, :]).astype(jnp.int32)
    position = jnp.arange(count, dtype=jnp.int32)
    earlier = (position[None, :] < position[:, None]).astype(jnp.int32)
    return jnp.sum(same_expert * earlier, axis=1)


def dot(a, b):
    return jnp.dot(a, b, preferred_element_type=F32)


def shift(value, by, groups):
    return lax.ppermute(value, "group", [(i, (i + by) % groups) for i in range(groups)])


def expert_kernel(count, *refs):
    rows, (w1, b1, w2), outs = refs[:count], refs[count : count + 3], refs[count + 3 :]
    size = rows[0].shape[0]
    value = jnp.concatenate([r[...] for r in rows], axis=0) if count > 1 else rows[0][...]
    hidden = jnp.maximum(dot(value, w1[...]) + b1[...], 0.0).astype(BF)
    terms = dot(hidden, w2[...]).astype(BF)
    for n in range(count):
        outs[n][...] = terms[n * size : (n + 1) * size]


def expert_terms(rows, w1, b1, w2):
    count, total = len(rows), sum(r.shape[0] for r in rows)
    depth, units = w1.shape
    width = w2.shape[1]
    spec = pl.BlockSpec(memory_space=pltpu.VMEM)
    return pl.pallas_call(
        lambda *refs: expert_kernel(count, *refs),
        out_shape=[jax.ShapeDtypeStruct((r.shape[0], width), BF) for r in rows],
        in_specs=[spec] * (count + 3),
        out_specs=[spec] * count,
        compiler_params=pltpu.CompilerParams(vmem_limit_bytes=24 * 2**20),
        cost_estimate=pl.CostEstimate(
            flops=2 * total * units * (depth + width),
            bytes_accessed=2 * (units * (depth + width) + total * (depth + width)),
            transcendentals=0,
        ),
    )(*rows, w1, b1, w2)


def ring_experts(own, experts_of, groups):
    half, middle = groups // 2, own.shape[0] // 2
    terms = {}
    held = {0: own}
    forward = backward = own
    for step in range(1, half):
        forward, backward = shift(forward, 1, groups), shift(backward, -1, groups)
        (forward, backward), done = lax.optimization_barrier(
            ((forward, backward), experts_of(list(held.values())))
        )
        terms.update(zip(held, done))
        held = {-step: forward, step: backward}
    far = [shift(forward[:middle], 1, groups), shift(backward[middle:], -1, groups)]
    far, done = lax.optimization_barrier((far, experts_of(list(held.values()))))
    terms.update(zip(held, done))
    terms[half] = experts_of(far)
    return terms


def ring_sum(terms, groups):
    half = groups // 2
    forward = shift(terms[half][0], 1, groups)
    backward = shift(terms[half][1], -1, groups)
    for offset in range(half - 1, 0, -1):
        ahead, behind = terms[offset].astype(F32), terms[-offset].astype(F32)
        if offset == half - 1:
            middle = forward.shape[0]
            ahead = jnp.concatenate([ahead[:middle] + forward.astype(F32), ahead[middle:]], axis=0)
            behind = jnp.concatenate([behind[:middle], behind[middle:] + backward.astype(F32)], axis=0)
        else:
            ahead, behind = ahead + forward.astype(F32), behind + backward.astype(F32)
        forward = shift(ahead.astype(BF), 1, groups)
        backward = shift(behind.astype(BF), -1, groups)
    return terms[0].astype(F32) + forward.astype(F32) + backward.astype(F32)


def on_device(
    tokens,
    expert_ids,
    gates,
    ln_gain,
    w_in,
    b_in,
    w_out,
    b_out,
    final_gain,
    w_cross,
    lengths,
    page_table,
    queries,
):
    rows_dev, width = tokens.shape
    experts = lax.axis_size("expert")
    groups = lax.axis_size("group")
    capacity = 2 * rows_dev // experts
    places = experts * capacity
    sentences = lengths.shape[1]
    head_size = queries.shape[1]
    column = lax.axis_index("expert")
    row = lax.axis_index("group")
    first, second = w_in[0], w_out[0]

    cross_cols = w_cross.shape[1]
    shard_rows = w_cross.shape[0]
    own_cross = jnp.concatenate([w_cross, queries], axis=1)
    own_cross = jnp.pad(own_cross, ((0, PAD_ROWS - shard_rows), (0, 0)))
    cross_rows = lax.all_gather(own_cross, "group", axis=0, tiled=False)

    normed = layer_norm(tokens.astype(F32), ln_gain).astype(BF)
    target = (expert_ids.reshape(-1) * capacity + slot_numbers(expert_ids)).reshape(rows_dev, 2)
    place_ids = jnp.arange(places, dtype=jnp.int32)
    goes = (
        (place_ids[:, None] == target[None, :, 0]) | (place_ids[:, None] == target[None, :, 1])
    ).astype(BF)
    outgoing = dot(goes, normed).astype(BF).reshape(experts, capacity, width)
    arrived = lax.all_to_all(outgoing, "expert", 0, 0, tiled=True).reshape(places, width)

    terms = ring_experts(arrived, lambda rows: expert_terms(rows, first, b_in, second), groups)
    cross_rows, _ = lax.optimization_barrier((cross_rows, terms[0]))
    cross_rows = cross_rows[:, :shard_rows]
    cross_rows = jnp.concatenate(
        [
            cross_rows[:, :, :cross_cols].transpose(1, 0, 2).reshape(shard_rows, -1),
            cross_rows[:, :, cross_cols:].transpose(1, 0, 2).reshape(shard_rows, -1),
        ],
        axis=1,
    )
    cross = lax.all_gather(cross_rows, "expert", axis=0, tiled=True)
    cross_weights = cross[:, : groups * cross_cols]

    sums = ring_sum(terms, groups)
    expert_out = (sums + b_out[0]).astype(BF).reshape(experts, capacity, width)
    returned = lax.all_to_all(expert_out, "expert", 0, 0, tiled=True).reshape(places, width)

    moe = 0.0
    for k in range(2):
        picks = (target[:, k][:, None] == place_ids[None, :]).astype(BF)
        moe = moe + gates[:, k][:, None] * dot(picks, returned)
    encoded = layer_norm(tokens.astype(F32) + moe, final_gain).astype(BF)

    keyvals = dot(encoded, cross_weights).astype(BF).reshape(rows_dev, groups, 2, head_size)
    block = column * groups + row
    own_lengths = lax.dynamic_slice_in_dim(lengths, block, 1, 0)[0]
    owners = lax.dynamic_slice_in_dim(page_table, block, 1, 0)[0]
    slots_dev = groups * sentences
    own_queries = jnp.concatenate(
        [
            lax.dynamic_slice(
                cross,
                (owners[k] * slots_dev + row * sentences + k, groups * cross_cols),
                (1, groups * head_size),
            )
            for k in range(sentences)
        ],
        axis=0,
    ).reshape(sentences, groups, head_size)
    scores = jnp.einsum(
        "khs,rhs->hkr", own_queries, keyvals[:, :, 0], preferred_element_type=F32
    ) / math.sqrt(head_size)
    ends = jnp.cumsum(own_lengths)
    starts = ends - own_lengths
    row_ids = jnp.arange(rows_dev, dtype=jnp.int32)
    visible = (row_ids[None, :] >= starts[:, None]) & (row_ids[None, :] < ends[:, None])
    scores = jnp.where(visible[None], scores, -jnp.inf)
    highest = jnp.max(scores, axis=-1, keepdims=True)
    exponent = jnp.exp(scores - highest)
    attention = (exponent / jnp.sum(exponent, axis=-1, keepdims=True)).astype(BF)
    own_context = jnp.einsum(
        "hkr,rhs->hks", attention, keyvals[:, :, 1], preferred_element_type=F32
    ).astype(BF)

    slots = lax.all_to_all(own_context, "group", 0, 0, tiled=True).reshape(slots_dev, head_size)
    column_ids = jnp.arange(experts, dtype=jnp.int32)
    column_owners = lax.dynamic_slice_in_dim(page_table, column * groups, groups, 0).reshape(-1)
    to_owner = (column_ids[:, None] == column_owners[None, :]).astype(BF)
    sent = dot(to_owner, slots).astype(BF).reshape(experts, 1, head_size)
    received = lax.all_to_all(sent, "expert", 0, 0, tiled=True).reshape(experts, head_size)
    first_owners = page_table[:groups].reshape(-1)
    source = lax.rem(column - first_owners + experts, experts)
    from_source = (source[:, None] == column_ids[None, :]).astype(BF)
    context = dot(from_source, received).astype(BF)
    return (encoded, context)


def solution(mesh):
    return jax.shard_map(
        on_device,
        mesh=mesh,
        in_specs=(
            P(("expert", "group"), None),
            P(("expert", "group"), None),
            P(("expert", "group"), None),
            P(),
            P("expert", None, "group"),
            P("expert", "group"),
            P("expert", "group", None),
            P("expert", None),
            P(),
            P("expert", "group"),
            P(),
            P(),
            P("expert", "group"),
        ),
        out_specs=(P(("expert", "group"), None), P("expert", "group")),
        check_vma=False,
    )
```

```python
import math

import jax
import jax.numpy as jnp
from jax import lax
from jax.experimental import pallas as pl
from jax.experimental.pallas import tpu as pltpu
from jax.sharding import PartitionSpec as P

EPSILON = 1e-05
PAD_ROWS = 192
BF = jnp.bfloat16
F32 = jnp.float32


def layer_norm(values, gain_row):
    average = jnp.mean(values, axis=-1, keepdims=True)
    centred = values - average
    variance = jnp.mean(centred * centred, axis=-1, keepdims=True)
    return centred * lax.rsqrt(variance + EPSILON) * gain_row


def dot(a, b):
    return jnp.dot(a, b, preferred_element_type=F32)


def shift(value, by, groups):
    return lax.ppermute(value, "group", [(i, (i + by) % groups) for i in range(groups)])


def whole(count):
    return [pl.BlockSpec(memory_space=pltpu.VMEM)] * count


def iota(shape, axis):
    return lax.broadcasted_iota(jnp.int32, shape, axis)


def dispatch_kernel(tokens, ids, gain, weights, asked, outgoing, picks, cross, rows_in, gain_in, sems):
    rows = tokens.shape[0]
    count, places = picks.shape
    capacity = count // rows
    cols = weights.shape[1]
    cross[...] = jnp.zeros_like(cross)
    copies = [
        pltpu.make_async_copy(tokens, rows_in, sems.at[0]),
        pltpu.make_async_copy(gain, gain_in, sems.at[1]),
        pltpu.make_async_copy(weights, cross.at[: weights.shape[0], :cols], sems.at[2]),
        pltpu.make_async_copy(asked, cross.at[: asked.shape[0], cols:], sems.at[3]),
    ]
    for copy in copies:
        copy.start()
    square = (count, count)
    along, down = iota(square, 1), iota(square, 0)
    spread = (iota((rows, count), 1) % rows == iota((rows, count), 0)).astype(BF)
    ids_along = dot(ids[...].astype(F32).astype(BF), spread).astype(jnp.int32)
    id_row = jnp.where(iota((1, count), 1) < rows, ids_along[0:1], ids_along[1:2])
    id_along = jnp.broadcast_to(id_row, square)
    id_down = jnp.sum(jnp.where(along == down, id_along, 0), axis=1, keepdims=True)
    key_along = 2 * (along % rows) + along // rows
    key_down = 2 * (down % rows) + down // rows
    same = id_along == id_down
    slot_along = jnp.sum((same & (key_down < key_along)).astype(jnp.int32), axis=0, keepdims=True)
    slot_down = jnp.sum((same & (key_along < key_down)).astype(jnp.int32), axis=1, keepdims=True)
    target_along = id_row * capacity + slot_along
    target_down = id_down * capacity + slot_down
    picks[...] = (target_down == iota((count, places), 1)).astype(BF)
    by_assignment = (target_along == iota((places, count), 0)).astype(BF)
    token_of = (iota((count, rows), 0) % rows == iota((count, rows), 1)).astype(BF)
    goes = dot(by_assignment, token_of).astype(BF)
    for copy in copies:
        copy.wait()
    normed = layer_norm(rows_in[...].astype(F32), gain_in[...]).astype(BF)
    outgoing[...] = dot(goes, normed).astype(BF)


def dispatch(tokens, expert_ids, gain, weights, asked, places):
    rows, width = tokens.shape
    count = expert_ids.size
    anywhere = pl.BlockSpec(memory_space=pl.ANY)
    return pl.pallas_call(
        dispatch_kernel,
        out_shape=[
            jax.ShapeDtypeStruct((places, width), BF),
            jax.ShapeDtypeStruct((count, places), BF),
            jax.ShapeDtypeStruct((PAD_ROWS, weights.shape[1] + asked.shape[1]), BF),
        ],
        in_specs=[anywhere, *whole(1), anywhere, anywhere, anywhere],
        out_specs=whole(3),
        scratch_shapes=[
            pltpu.VMEM((rows, width), BF),
            pltpu.VMEM((1, width), F32),
            pltpu.SemaphoreType.DMA((4,)),
        ],
        compiler_params=pltpu.CompilerParams(vmem_limit_bytes=40 * 2**20),
    )(tokens, expert_ids.T, gain.reshape(1, width), weights, asked)


def tail_kernel(
    tokens, returned, picks, gates, gain, cross, asked, marks, encoded, context, weights, sems
):
    rows = tokens.shape[0]
    count, head_size = context.shape
    heads = weights.shape[0]
    sentences = count // heads
    step = 2 * head_size
    copies = [
        pltpu.make_async_copy(cross.at[:, h * step : (h + 1) * step], weights.at[h], sems.at[h])
        for h in range(heads)
    ]
    for copy in copies:
        copy.start()
    picked = dot(picks[...], returned[...])
    moe = gates[:, 0:1] * picked[:rows] + gates[:, 1:2] * picked[rows:]
    value = layer_norm(tokens[...].astype(F32) + moe, gain[...]).astype(BF)
    encoded[...] = value
    head_of = iota((count, head_size), 0) // sentences
    scores = jnp.zeros((count, rows), F32)
    values = []
    for h in range(heads):
        copies[h].wait()
        both = dot(value, weights[h]).astype(BF)
        query = jnp.where(head_of == h, asked[...], 0).astype(BF)
        scores += lax.dot_general(
            query, both[:, :head_size], (((1,), (1,)), ((), ())), preferred_element_type=F32
        )
        values.append(both[:, head_size:])
    scores = scores / math.sqrt(head_size)
    row_ids = iota((count, rows), 1)
    visible = (row_ids >= marks[:, 0:1]) & (row_ids < marks[:, 1:2])
    scores = jnp.where(visible, scores, -jnp.inf)
    exponent = jnp.exp(scores - jnp.max(scores, axis=-1, keepdims=True))
    attention = (exponent / jnp.sum(exponent, axis=-1, keepdims=True)).astype(BF)
    result = jnp.zeros((count, head_size), F32)
    for h in range(heads):
        result = jnp.where(head_of == h, dot(attention, values[h]), result)
    context[...] = result.astype(BF)


def tail(tokens, returned, picks, gates, gain, cross, asked, marks, heads):
    rows, width = tokens.shape
    step = 2 * asked.shape[1]
    specs = whole(8)
    specs[5] = pl.BlockSpec(memory_space=pl.ANY)
    return pl.pallas_call(
        tail_kernel,
        out_shape=[jax.ShapeDtypeStruct((rows, width), BF), jax.ShapeDtypeStruct(asked.shape, BF)],
        in_specs=specs,
        out_specs=whole(2),
        scratch_shapes=[
            pltpu.VMEM((heads, width, step), BF),
            pltpu.SemaphoreType.DMA((heads,)),
        ],
        compiler_params=pltpu.CompilerParams(vmem_limit_bytes=40 * 2**20),
        cost_estimate=pl.CostEstimate(
            flops=2 * rows * width * heads * step,
            bytes_accessed=2 * width * heads * step,
            transcendentals=0,
        ),
    )(tokens, returned, picks, gates, gain.reshape(1, width), cross, asked, marks)


def expert_kernel(count, *refs):
    rows, (w1, b1, w2), outs = refs[:count], refs[count : count + 3], refs[count + 3 :]
    size = rows[0].shape[0]
    value = jnp.concatenate([r[...] for r in rows], axis=0) if count > 1 else rows[0][...]
    hidden = jnp.maximum(dot(value, w1[...]) + b1[...], 0.0).astype(BF)
    terms = dot(hidden, w2[...]).astype(BF)
    for n in range(count):
        outs[n][...] = terms[n * size : (n + 1) * size]


def expert_terms(rows, w1, b1, w2):
    count, total = len(rows), sum(r.shape[0] for r in rows)
    depth, units = w1.shape
    width = w2.shape[1]
    spec = pl.BlockSpec(memory_space=pltpu.VMEM)
    return pl.pallas_call(
        lambda *refs: expert_kernel(count, *refs),
        out_shape=[jax.ShapeDtypeStruct((r.shape[0], width), BF) for r in rows],
        in_specs=[spec] * (count + 3),
        out_specs=[spec] * count,
        compiler_params=pltpu.CompilerParams(vmem_limit_bytes=24 * 2**20),
        cost_estimate=pl.CostEstimate(
            flops=2 * total * units * (depth + width),
            bytes_accessed=2 * (units * (depth + width) + total * (depth + width)),
            transcendentals=0,
        ),
    )(*rows, w1, b1, w2)


def ring_experts(own, experts_of, groups):
    half, middle = groups // 2, own.shape[0] // 2
    terms = {}
    held = {0: own}
    forward = backward = own
    for step in range(1, half):
        forward, backward = shift(forward, 1, groups), shift(backward, -1, groups)
        (forward, backward), done = lax.optimization_barrier(
            ((forward, backward), experts_of(list(held.values())))
        )
        terms.update(zip(held, done))
        held = {-step: forward, step: backward}
    far = [shift(forward[:middle], 1, groups), shift(backward[middle:], -1, groups)]
    far, done = lax.optimization_barrier((far, experts_of(list(held.values()))))
    terms.update(zip(held, done))
    terms[half] = experts_of(far)
    return terms


def ring_sum(terms, groups):
    half = groups // 2
    forward = shift(terms[half][0], 1, groups)
    backward = shift(terms[half][1], -1, groups)
    for offset in range(half - 1, 0, -1):
        ahead, behind = terms[offset].astype(F32), terms[-offset].astype(F32)
        if offset == half - 1:
            middle = forward.shape[0]
            ahead = jnp.concatenate([ahead[:middle] + forward.astype(F32), ahead[middle:]], axis=0)
            behind = jnp.concatenate([behind[:middle], behind[middle:] + backward.astype(F32)], axis=0)
        else:
            ahead, behind = ahead + forward.astype(F32), behind + backward.astype(F32)
        forward = shift(ahead.astype(BF), 1, groups)
        backward = shift(behind.astype(BF), -1, groups)
    return terms[0].astype(F32) + forward.astype(F32) + backward.astype(F32)


def on_device(
    tokens,
    expert_ids,
    gates,
    ln_gain,
    w_in,
    b_in,
    w_out,
    b_out,
    final_gain,
    w_cross,
    lengths,
    page_table,
    queries,
):
    rows_dev, width = tokens.shape
    experts = lax.axis_size("expert")
    groups = lax.axis_size("group")
    capacity = 2 * rows_dev // experts
    places = experts * capacity
    sentences = lengths.shape[1]
    head_size = queries.shape[1]
    column = lax.axis_index("expert")
    row = lax.axis_index("group")
    first, second = w_in[0], w_out[0]

    cross_cols = w_cross.shape[1]
    shard_rows = w_cross.shape[0]
    outgoing, picks, own_cross = dispatch(tokens, expert_ids, ln_gain, w_cross, queries, places)
    cross_rows = lax.all_gather(own_cross, "group", axis=0, tiled=False)
    outgoing = outgoing.reshape(experts, capacity, width)
    arrived = lax.all_to_all(outgoing, "expert", 0, 0, tiled=True).reshape(places, width)

    terms = ring_experts(arrived, lambda rows: expert_terms(rows, first, b_in, second), groups)
    cross_rows, _ = lax.optimization_barrier((cross_rows, terms[0]))
    cross_rows = cross_rows[:, :shard_rows]
    cross_rows = jnp.concatenate(
        [
            cross_rows[:, :, :cross_cols].transpose(1, 0, 2).reshape(shard_rows, -1),
            cross_rows[:, :, cross_cols:].transpose(1, 0, 2).reshape(shard_rows, -1),
        ],
        axis=1,
    )
    cross = lax.all_gather(cross_rows, "expert", axis=0, tiled=True)

    sums = ring_sum(terms, groups)
    expert_out = (sums + b_out[0]).astype(BF).reshape(experts, capacity, width)
    returned = lax.all_to_all(expert_out, "expert", 0, 0, tiled=True).reshape(places, width)

    block = column * groups + row
    own_lengths = lax.dynamic_slice_in_dim(lengths, block, 1, 0)[0]
    owners = lax.dynamic_slice_in_dim(page_table, block, 1, 0)[0]
    slots_dev = groups * sentences
    asked = jnp.concatenate(
        [
            lax.dynamic_slice(
                cross,
                (owners[k] * slots_dev + row * sentences + k, groups * cross_cols),
                (1, groups * head_size),
            )
            for k in range(sentences)
        ],
        axis=0,
    )
    asked = asked.reshape(sentences, groups, head_size).transpose(1, 0, 2).reshape(-1, head_size)
    ends = jnp.cumsum(own_lengths)
    marks = jnp.tile(jnp.stack([ends - own_lengths, ends], axis=1), (groups, 1))

    encoded, own_context = tail(
        tokens, returned, picks, gates, final_gain, cross, asked, marks, groups
    )
    own_context = own_context.reshape(groups, sentences, head_size)

    slots = lax.all_to_all(own_context, "group", 0, 0, tiled=True).reshape(slots_dev, head_size)
    column_ids = jnp.arange(experts, dtype=jnp.int32)
    column_owners = lax.dynamic_slice_in_dim(page_table, column * groups, groups, 0).reshape(-1)
    to_owner = (column_ids[:, None] == column_owners[None, :]).astype(BF)
    sent = dot(to_owner, slots).astype(BF).reshape(experts, 1, head_size)
    received = lax.all_to_all(sent, "expert", 0, 0, tiled=True).reshape(experts, head_size)
    first_owners = page_table[:groups].reshape(-1)
    source = lax.rem(column - first_owners + experts, experts)
    from_source = (source[:, None] == column_ids[None, :]).astype(BF)
    context = dot(from_source, received).astype(BF)
    return (encoded, context)


def solution(mesh):
    return jax.shard_map(
        on_device,
        mesh=mesh,
        in_specs=(
            P(("expert", "group"), None),
            P(("expert", "group"), None),
            P(("expert", "group"), None),
            P(),
            P("expert", None, "group"),
            P("expert", "group"),
            P("expert", "group", None),
            P("expert", None),
            P(),
            P("expert", "group"),
            P(),
            P(),
            P("expert", "group"),
        ),
        out_specs=(P(("expert", "group"), None), P("expert", "group")),
        check_vma=False,
    )
```

```python
import math

import jax
import jax.numpy as jnp
from jax import lax
from jax.experimental import pallas as pl
from jax.experimental.pallas import tpu as pltpu
from jax.sharding import PartitionSpec as P

EPSILON = 1e-05
PAD_ROWS = 192
BF = jnp.bfloat16
F32 = jnp.float32


def layer_norm(values, gain_row):
    average = jnp.mean(values, axis=-1, keepdims=True)
    centred = values - average
    variance = jnp.mean(centred * centred, axis=-1, keepdims=True)
    return centred * lax.rsqrt(variance + EPSILON) * gain_row


def dot(a, b):
    return jnp.dot(a, b, preferred_element_type=F32)


def shift(value, by, groups):
    return lax.ppermute(value, "group", [(i, (i + by) % groups) for i in range(groups)])


def whole(count):
    return [pl.BlockSpec(memory_space=pltpu.VMEM)] * count


def iota(shape, axis):
    return lax.broadcasted_iota(jnp.int32, shape, axis)


def dispatch_kernel(tokens, ids, gain, weights, asked, outgoing, picks, cross, rows_in, gain_in, sems):
    rows = tokens.shape[0]
    count, places = picks.shape
    capacity = count // rows
    cols = weights.shape[1]
    cross[...] = jnp.zeros_like(cross)
    copies = [
        pltpu.make_async_copy(tokens, rows_in, sems.at[0]),
        pltpu.make_async_copy(gain, gain_in, sems.at[1]),
        pltpu.make_async_copy(weights, cross.at[: weights.shape[0], :cols], sems.at[2]),
        pltpu.make_async_copy(asked, cross.at[: asked.shape[0], cols:], sems.at[3]),
    ]
    for copy in copies:
        copy.start()
    square = (count, count)
    along, down = iota(square, 1), iota(square, 0)
    spread = (iota((rows, count), 1) % rows == iota((rows, count), 0)).astype(BF)
    ids_along = dot(ids[...].astype(F32).astype(BF), spread).astype(jnp.int32)
    id_row = jnp.where(iota((1, count), 1) < rows, ids_along[0:1], ids_along[1:2])
    id_along = jnp.broadcast_to(id_row, square)
    id_down = jnp.sum(jnp.where(along == down, id_along, 0), axis=1, keepdims=True)
    key_along = 2 * (along % rows) + along // rows
    key_down = 2 * (down % rows) + down // rows
    same = id_along == id_down
    slot_along = jnp.sum((same & (key_down < key_along)).astype(jnp.int32), axis=0, keepdims=True)
    slot_down = jnp.sum((same & (key_along < key_down)).astype(jnp.int32), axis=1, keepdims=True)
    target_along = id_row * capacity + slot_along
    target_down = id_down * capacity + slot_down
    picks[...] = (target_down == iota((count, places), 1)).astype(BF)
    by_assignment = (target_along == iota((places, count), 0)).astype(BF)
    token_of = (iota((count, rows), 0) % rows == iota((count, rows), 1)).astype(BF)
    goes = dot(by_assignment, token_of).astype(BF)
    for copy in copies:
        copy.wait()
    normed = layer_norm(rows_in[...].astype(F32), gain_in[...]).astype(BF)
    outgoing[...] = dot(goes, normed).astype(BF)


def dispatch(tokens, expert_ids, gain, weights, asked, places):
    rows, width = tokens.shape
    count = expert_ids.size
    anywhere = pl.BlockSpec(memory_space=pl.ANY)
    return pl.pallas_call(
        dispatch_kernel,
        out_shape=[
            jax.ShapeDtypeStruct((places, width), BF),
            jax.ShapeDtypeStruct((count, places), BF),
            jax.ShapeDtypeStruct((PAD_ROWS, weights.shape[1] + asked.shape[1]), BF),
        ],
        in_specs=[anywhere, *whole(1), anywhere, anywhere, anywhere],
        out_specs=whole(3),
        scratch_shapes=[
            pltpu.VMEM((rows, width), BF),
            pltpu.VMEM((1, width), F32),
            pltpu.SemaphoreType.DMA((4,)),
        ],
    )(tokens, expert_ids.T, gain.reshape(1, width), weights, asked)


def tail_kernel(
    info, tokens, returned, picks, gates, gain, cross, encoded, context, weights, asked, sems
):
    rows = tokens.shape[0]
    count, head_size = context.shape
    heads = weights.shape[0]
    sentences = count // heads
    step = 2 * head_size
    block = asked.shape[1]
    copies = [
        pltpu.make_async_copy(
            cross.at[pl.ds(pl.multiple_of(info[0, k] // block * block, block), block), heads * step :],
            asked.at[k],
            sems.at[heads + k],
        )
        for k in range(sentences)
    ] + [
        pltpu.make_async_copy(cross.at[:, h * step : (h + 1) * step], weights.at[h], sems.at[h])
        for h in range(heads)
    ]
    for copy in copies:
        copy.start()
    picked = dot(picks[...], returned[...])
    moe = gates[:, 0:1] * picked[:rows] + gates[:, 1:2] * picked[rows:]
    value = layer_norm(tokens[...].astype(F32) + moe, gain[...]).astype(BF)
    encoded[...] = value
    sentence_of = iota((count, 1), 0) % sentences
    head_of = iota((count, head_size), 0) // sentences
    begin = jnp.zeros((count, 1), jnp.int32)
    end = jnp.zeros((count, 1), jnp.int32)
    queries = jnp.zeros((count, heads * head_size), F32)
    for k in range(sentences):
        begin = jnp.where(sentence_of == k, info[1, k], begin)
        end = jnp.where(sentence_of == k, info[2, k], end)
        copies[k].wait()
        chosen = (iota((count, block), 1) == info[0, k] % block) & (iota((count, block), 0) % sentences == k)
        queries += dot(chosen.astype(BF), asked[k])
    queries = queries.astype(BF)
    scores = jnp.zeros((count, rows), F32)
    values = []
    for h in range(heads):
        copies[sentences + h].wait()
        both = dot(value, weights[h]).astype(BF)
        query = jnp.where(head_of == h, queries[:, h * head_size : (h + 1) * head_size], 0).astype(BF)
        scores += lax.dot_general(
            query, both[:, :head_size], (((1,), (1,)), ((), ())), preferred_element_type=F32
        )
        values.append(both[:, head_size:])
    scores = scores / math.sqrt(head_size)
    row_ids = iota((count, rows), 1)
    visible = (row_ids >= begin) & (row_ids < end)
    scores = jnp.where(visible, scores, -jnp.inf)
    exponent = jnp.exp(scores - jnp.max(scores, axis=-1, keepdims=True))
    attention = (exponent / jnp.sum(exponent, axis=-1, keepdims=True)).astype(BF)
    result = jnp.zeros((count, head_size), F32)
    for h in range(heads):
        result = jnp.where(head_of == h, dot(attention, values[h]), result)
    context[...] = result.astype(BF)


def tail(info, tokens, returned, picks, gates, gain, cross, heads, head_size):
    rows, width = tokens.shape
    step = 2 * head_size
    sentences = info.shape[1]
    specs = whole(7)
    specs[0] = pl.BlockSpec(memory_space=pltpu.SMEM)
    specs[6] = pl.BlockSpec(memory_space=pl.ANY)
    return pl.pallas_call(
        tail_kernel,
        out_shape=[
            jax.ShapeDtypeStruct((rows, width), BF),
            jax.ShapeDtypeStruct((heads * sentences, head_size), BF),
        ],
        in_specs=specs,
        out_specs=whole(2),
        scratch_shapes=[
            pltpu.VMEM((heads, width, step), BF),
            pltpu.VMEM((sentences, 16, heads * head_size), BF),
            pltpu.SemaphoreType.DMA((heads + sentences,)),
        ],
        compiler_params=pltpu.CompilerParams(vmem_limit_bytes=60 * 2**20),
        cost_estimate=pl.CostEstimate(
            flops=2 * rows * width * heads * step,
            bytes_accessed=2 * width * heads * step,
            transcendentals=0,
        ),
    )(info, tokens, returned, picks, gates, gain.reshape(1, width), cross)


def expert_kernel(count, *refs):
    rows, (w1, b1, w2), outs = refs[:count], refs[count : count + 3], refs[count + 3 :]
    size = rows[0].shape[0]
    value = jnp.concatenate([r[...] for r in rows], axis=0) if count > 1 else rows[0][...]
    hidden = jnp.maximum(dot(value, w1[...]) + b1[...], 0.0).astype(BF)
    terms = dot(hidden, w2[...]).astype(BF)
    for n in range(count):
        outs[n][...] = terms[n * size : (n + 1) * size]


def expert_terms(rows, w1, b1, w2):
    count, total = len(rows), sum(r.shape[0] for r in rows)
    depth, units = w1.shape
    width = w2.shape[1]
    spec = pl.BlockSpec(memory_space=pltpu.VMEM)
    return pl.pallas_call(
        lambda *refs: expert_kernel(count, *refs),
        out_shape=[jax.ShapeDtypeStruct((r.shape[0], width), BF) for r in rows],
        in_specs=[spec] * (count + 3),
        out_specs=[spec] * count,
        compiler_params=pltpu.CompilerParams(vmem_limit_bytes=24 * 2**20),
        cost_estimate=pl.CostEstimate(
            flops=2 * total * units * (depth + width),
            bytes_accessed=2 * (units * (depth + width) + total * (depth + width)),
            transcendentals=0,
        ),
    )(*rows, w1, b1, w2)


def ring_experts(own, experts_of, groups):
    half, middle = groups // 2, own.shape[0] // 2
    terms = {}
    held = {0: own}
    forward = backward = own
    for step in range(1, half):
        forward, backward = shift(forward, 1, groups), shift(backward, -1, groups)
        (forward, backward), done = lax.optimization_barrier(
            ((forward, backward), experts_of(list(held.values())))
        )
        terms.update(zip(held, done))
        held = {-step: forward, step: backward}
    far = [shift(forward[:middle], 1, groups), shift(backward[middle:], -1, groups)]
    far, done = lax.optimization_barrier((far, experts_of(list(held.values()))))
    terms.update(zip(held, done))
    terms[half] = experts_of(far)
    return terms


def ring_sum(terms, groups):
    half = groups // 2
    forward = shift(terms[half][0], 1, groups)
    backward = shift(terms[half][1], -1, groups)
    for offset in range(half - 1, 0, -1):
        ahead, behind = terms[offset].astype(F32), terms[-offset].astype(F32)
        if offset == half - 1:
            middle = forward.shape[0]
            ahead = jnp.concatenate([ahead[:middle] + forward.astype(F32), ahead[middle:]], axis=0)
            behind = jnp.concatenate([behind[:middle], behind[middle:] + backward.astype(F32)], axis=0)
        else:
            ahead, behind = ahead + forward.astype(F32), behind + backward.astype(F32)
        forward = shift(ahead.astype(BF), 1, groups)
        backward = shift(behind.astype(BF), -1, groups)
    return terms[0].astype(F32) + forward.astype(F32) + backward.astype(F32)


def on_device(
    tokens,
    expert_ids,
    gates,
    ln_gain,
    w_in,
    b_in,
    w_out,
    b_out,
    final_gain,
    w_cross,
    lengths,
    page_table,
    queries,
):
    rows_dev, width = tokens.shape
    experts = lax.axis_size("expert")
    groups = lax.axis_size("group")
    capacity = 2 * rows_dev // experts
    places = experts * capacity
    sentences = lengths.shape[1]
    head_size = queries.shape[1]
    column = lax.axis_index("expert")
    row = lax.axis_index("group")
    first, second = w_in[0], w_out[0]

    cross_cols = w_cross.shape[1]
    shard_rows = w_cross.shape[0]
    outgoing, picks, own_cross = dispatch(tokens, expert_ids, ln_gain, w_cross, queries, places)
    cross_rows = lax.all_gather(own_cross, "group", axis=0, tiled=False)
    outgoing = outgoing.reshape(experts, capacity, width)
    arrived = lax.all_to_all(outgoing, "expert", 0, 0, tiled=True).reshape(places, width)

    terms = ring_experts(arrived, lambda rows: expert_terms(rows, first, b_in, second), groups)
    cross_rows, _ = lax.optimization_barrier((cross_rows, terms[0]))
    cross_rows = cross_rows[:, :shard_rows]
    cross_rows = jnp.concatenate(
        [
            cross_rows[:, :, :cross_cols].transpose(1, 0, 2).reshape(shard_rows, -1),
            cross_rows[:, :, cross_cols:].transpose(1, 0, 2).reshape(shard_rows, -1),
        ],
        axis=1,
    )
    cross = lax.all_gather(cross_rows, "expert", axis=0, tiled=True)

    sums = ring_sum(terms, groups)
    expert_out = (sums + b_out[0]).astype(BF).reshape(experts, capacity, width)
    returned = lax.all_to_all(expert_out, "expert", 0, 0, tiled=True).reshape(places, width)

    block = column * groups + row
    own_lengths = lax.dynamic_slice_in_dim(lengths, block, 1, 0)[0]
    owners = lax.dynamic_slice_in_dim(page_table, block, 1, 0)[0]
    slots_dev = groups * sentences
    ends = jnp.cumsum(own_lengths)
    query_rows = owners * slots_dev + row * sentences + jnp.arange(sentences, dtype=jnp.int32)
    info = jnp.stack([query_rows, ends - own_lengths, ends])

    encoded, own_context = tail(
        info, tokens, returned, picks, gates, final_gain, cross, groups, head_size
    )
    own_context = own_context.reshape(groups, sentences, head_size)

    slots = lax.all_to_all(own_context, "group", 0, 0, tiled=True).reshape(slots_dev, head_size)
    column_ids = jnp.arange(experts, dtype=jnp.int32)
    column_owners = lax.dynamic_slice_in_dim(page_table, column * groups, groups, 0).reshape(-1)
    to_owner = (column_ids[:, None] == column_owners[None, :]).astype(BF)
    sent = dot(to_owner, slots).astype(BF).reshape(experts, 1, head_size)
    received = lax.all_to_all(sent, "expert", 0, 0, tiled=True).reshape(experts, head_size)
    first_owners = page_table[:groups].reshape(-1)
    source = lax.rem(column - first_owners + experts, experts)
    from_source = (source[:, None] == column_ids[None, :]).astype(BF)
    context = dot(from_source, received).astype(BF)
    return (encoded, context)


def solution(mesh):
    return jax.shard_map(
        on_device,
        mesh=mesh,
        in_specs=(
            P(("expert", "group"), None),
            P(("expert", "group"), None),
            P(("expert", "group"), None),
            P(),
            P("expert", None, "group"),
            P("expert", "group"),
            P("expert", "group", None),
            P("expert", None),
            P(),
            P("expert", "group"),
            P(),
            P(),
            P("expert", "group"),
        ),
        out_specs=(P(("expert", "group"), None), P("expert", "group")),
        check_vma=False,
    )
```

```python
import math

import jax
import jax.numpy as jnp
from jax import lax
from jax.experimental import pallas as pl
from jax.experimental.pallas import tpu as pltpu
from jax.sharding import PartitionSpec as P

EPSILON = 1e-05
PAD_ROWS = 192
BF = jnp.bfloat16
F32 = jnp.float32


def layer_norm(values, gain_row):
    average = jnp.mean(values, axis=-1, keepdims=True)
    centred = values - average
    variance = jnp.mean(centred * centred, axis=-1, keepdims=True)
    return centred * lax.rsqrt(variance + EPSILON) * gain_row


def dot(a, b):
    return jnp.dot(a, b, preferred_element_type=F32)


def shift(value, by, groups):
    return lax.ppermute(value, "group", [(i, (i + by) % groups) for i in range(groups)])


def whole(count):
    return [pl.BlockSpec(memory_space=pltpu.VMEM)] * count


def iota(shape, axis):
    return lax.broadcasted_iota(jnp.int32, shape, axis)


def dispatch_kernel(tokens, ids, gain, weights, asked, outgoing, picks, cross, rows_in, gain_in, sems):
    rows = tokens.shape[0]
    count, places = picks.shape
    capacity = count // rows
    cols = weights.shape[1]
    cross[...] = jnp.zeros_like(cross)
    copies = [
        pltpu.make_async_copy(tokens, rows_in, sems.at[0]),
        pltpu.make_async_copy(gain, gain_in, sems.at[1]),
        pltpu.make_async_copy(weights, cross.at[: weights.shape[0], :cols], sems.at[2]),
        pltpu.make_async_copy(asked, cross.at[: asked.shape[0], cols:], sems.at[3]),
    ]
    for copy in copies:
        copy.start()
    square = (count, count)
    along, down = iota(square, 1), iota(square, 0)
    spread = (iota((rows, count), 1) % rows == iota((rows, count), 0)).astype(BF)
    ids_along = dot(ids[...].astype(F32).astype(BF), spread).astype(jnp.int32)
    id_row = jnp.where(iota((1, count), 1) < rows, ids_along[0:1], ids_along[1:2])
    id_along = jnp.broadcast_to(id_row, square)
    id_down = jnp.sum(jnp.where(along == down, id_along, 0), axis=1, keepdims=True)
    key_along = 2 * (along % rows) + along // rows
    key_down = 2 * (down % rows) + down // rows
    same = id_along == id_down
    slot_along = jnp.sum((same & (key_down < key_along)).astype(jnp.int32), axis=0, keepdims=True)
    slot_down = jnp.sum((same & (key_along < key_down)).astype(jnp.int32), axis=1, keepdims=True)
    target_along = id_row * capacity + slot_along
    target_down = id_down * capacity + slot_down
    picks[...] = (target_down == iota((count, places), 1)).astype(BF)
    by_assignment = (target_along == iota((places, count), 0)).astype(BF)
    token_of = (iota((count, rows), 0) % rows == iota((count, rows), 1)).astype(BF)
    goes = dot(by_assignment, token_of).astype(BF)
    for copy in copies:
        copy.wait()
    normed = layer_norm(rows_in[...].astype(F32), gain_in[...]).astype(BF)
    outgoing[...] = dot(goes, normed).astype(BF).reshape(outgoing.shape)


def dispatch(tokens, expert_ids, gain, weights, asked, places):
    rows, width = tokens.shape
    count = expert_ids.size
    capacity = count // rows
    anywhere = pl.BlockSpec(memory_space=pl.ANY)
    return pl.pallas_call(
        dispatch_kernel,
        out_shape=[
            jax.ShapeDtypeStruct((places // capacity, capacity, width), BF),
            jax.ShapeDtypeStruct((count, places), BF),
            jax.ShapeDtypeStruct((PAD_ROWS, weights.shape[1] + asked.shape[1]), BF),
        ],
        in_specs=[anywhere, *whole(1), anywhere, anywhere, anywhere],
        out_specs=whole(3),
        scratch_shapes=[
            pltpu.VMEM((rows, width), BF),
            pltpu.VMEM((1, width), F32),
            pltpu.SemaphoreType.DMA((4,)),
        ],
    )(tokens, expert_ids.T, gain.reshape(1, width), weights, asked)


def side_by_side_kernel(cols, parts, out):
    rows = out.shape[0]
    count, _, total = parts.shape
    rest = total - cols
    for n in range(count):
        out[:, n * cols : (n + 1) * cols] = parts[n, :rows, :cols]
        out[:, count * cols + n * rest : count * cols + (n + 1) * rest] = parts[n, :rows, cols:]


def side_by_side(parts, rows, cols):
    return pl.pallas_call(
        lambda *refs: side_by_side_kernel(cols, *refs),
        out_shape=jax.ShapeDtypeStruct((rows, parts.shape[0] * parts.shape[2]), BF),
        in_specs=whole(1),
        out_specs=pl.BlockSpec(memory_space=pltpu.VMEM),
        compiler_params=pltpu.CompilerParams(vmem_limit_bytes=4 * 2**20),
    )(parts)


def tail_kernel(
    info, tokens, returned, picks, gates, gain, cross, encoded, context, weights, asked, sems
):
    rows = tokens.shape[0]
    count, head_size = context.shape
    heads = weights.shape[0]
    sentences = count // heads
    step = 2 * head_size
    block = asked.shape[1]
    copies = [
        pltpu.make_async_copy(
            cross.at[pl.ds(pl.multiple_of(info[0, k] // block * block, block), block), heads * step :],
            asked.at[k],
            sems.at[heads + k],
        )
        for k in range(sentences)
    ] + [
        pltpu.make_async_copy(cross.at[:, h * step : (h + 1) * step], weights.at[h], sems.at[h])
        for h in range(heads)
    ]
    for copy in copies:
        copy.start()
    picked = dot(picks[...], returned[...].reshape(picks.shape[1], returned.shape[2]))
    moe = gates[:, 0:1] * picked[:rows] + gates[:, 1:2] * picked[rows:]
    value = layer_norm(tokens[...].astype(F32) + moe, gain[...]).astype(BF)
    encoded[...] = value
    sentence_of = iota((count, 1), 0) % sentences
    head_of = iota((count, head_size), 0) // sentences
    begin = jnp.zeros((count, 1), jnp.int32)
    end = jnp.zeros((count, 1), jnp.int32)
    queries = jnp.zeros((count, heads * head_size), F32)
    for k in range(sentences):
        begin = jnp.where(sentence_of == k, info[1, k], begin)
        end = jnp.where(sentence_of == k, info[2, k], end)
        copies[k].wait()
        chosen = (iota((count, block), 1) == info[0, k] % block) & (iota((count, block), 0) % sentences == k)
        queries += dot(chosen.astype(BF), asked[k])
    queries = queries.astype(BF)
    scores = jnp.zeros((count, rows), F32)
    values = []
    for h in range(heads):
        copies[sentences + h].wait()
        both = dot(value, weights[h]).astype(BF)
        query = jnp.where(head_of == h, queries[:, h * head_size : (h + 1) * head_size], 0).astype(BF)
        scores += lax.dot_general(
            query, both[:, :head_size], (((1,), (1,)), ((), ())), preferred_element_type=F32
        )
        values.append(both[:, head_size:])
    scores = scores / math.sqrt(head_size)
    row_ids = iota((count, rows), 1)
    visible = (row_ids >= begin) & (row_ids < end)
    scores = jnp.where(visible, scores, -jnp.inf)
    exponent = jnp.exp(scores - jnp.max(scores, axis=-1, keepdims=True))
    attention = (exponent / jnp.sum(exponent, axis=-1, keepdims=True)).astype(BF)
    result = jnp.zeros((count, head_size), F32)
    for h in range(heads):
        result = jnp.where(head_of == h, dot(attention, values[h]), result)
    context[...] = result.astype(BF)


def tail(info, tokens, returned, picks, gates, gain, cross, heads, head_size):
    rows, width = tokens.shape
    step = 2 * head_size
    sentences = info.shape[1]
    specs = whole(7)
    specs[0] = pl.BlockSpec(memory_space=pltpu.SMEM)
    specs[6] = pl.BlockSpec(memory_space=pl.ANY)
    return pl.pallas_call(
        tail_kernel,
        out_shape=[
            jax.ShapeDtypeStruct((rows, width), BF),
            jax.ShapeDtypeStruct((heads * sentences, head_size), BF),
        ],
        in_specs=specs,
        out_specs=whole(2),
        scratch_shapes=[
            pltpu.VMEM((heads, width, step), BF),
            pltpu.VMEM((sentences, 16, heads * head_size), BF),
            pltpu.SemaphoreType.DMA((heads + sentences,)),
        ],
        compiler_params=pltpu.CompilerParams(vmem_limit_bytes=60 * 2**20),
        cost_estimate=pl.CostEstimate(
            flops=2 * rows * width * heads * step,
            bytes_accessed=2 * width * heads * step,
            transcendentals=0,
        ),
    )(info, tokens, returned, picks, gates, gain.reshape(1, width), cross)


def expert_kernel(count, *refs):
    rows, (w1, b1, w2), outs = refs[:count], refs[count : count + 3], refs[count + 3 :]
    size = rows[0].shape[0]
    value = jnp.concatenate([r[...] for r in rows], axis=0) if count > 1 else rows[0][...]
    hidden = jnp.maximum(dot(value, w1[...]) + b1[...], 0.0).astype(BF)
    terms = dot(hidden, w2[...]).astype(BF)
    for n in range(count):
        outs[n][...] = terms[n * size : (n + 1) * size]


def expert_terms(rows, w1, b1, w2):
    count, total = len(rows), sum(r.shape[0] for r in rows)
    depth, units = w1.shape
    width = w2.shape[1]
    spec = pl.BlockSpec(memory_space=pltpu.VMEM)
    return pl.pallas_call(
        lambda *refs: expert_kernel(count, *refs),
        out_shape=[jax.ShapeDtypeStruct((r.shape[0], width), BF) for r in rows],
        in_specs=[spec] * (count + 3),
        out_specs=[spec] * count,
        compiler_params=pltpu.CompilerParams(vmem_limit_bytes=24 * 2**20),
        cost_estimate=pl.CostEstimate(
            flops=2 * total * units * (depth + width),
            bytes_accessed=2 * (units * (depth + width) + total * (depth + width)),
            transcendentals=0,
        ),
    )(*rows, w1, b1, w2)


def ring_experts(own, experts_of, groups):
    half, middle = groups // 2, own.shape[0] // 2
    terms = {}
    held = {0: own}
    forward = backward = own
    for step in range(1, half):
        forward, backward = shift(forward, 1, groups), shift(backward, -1, groups)
        (forward, backward), done = lax.optimization_barrier(
            ((forward, backward), experts_of(list(held.values())))
        )
        terms.update(zip(held, done))
        held = {-step: forward, step: backward}
    far = [shift(forward[:middle], 1, groups), shift(backward[middle:], -1, groups)]
    far, done = lax.optimization_barrier((far, experts_of(list(held.values()))))
    terms.update(zip(held, done))
    terms[half] = experts_of(far)
    return terms


def ring_sum(terms, groups):
    half = groups // 2
    forward = shift(terms[half][0], 1, groups)
    backward = shift(terms[half][1], -1, groups)
    for offset in range(half - 1, 0, -1):
        ahead, behind = terms[offset].astype(F32), terms[-offset].astype(F32)
        if offset == half - 1:
            middle = forward.shape[0]
            ahead = jnp.concatenate([ahead[:middle] + forward.astype(F32), ahead[middle:]], axis=0)
            behind = jnp.concatenate([behind[:middle], behind[middle:] + backward.astype(F32)], axis=0)
        else:
            ahead, behind = ahead + forward.astype(F32), behind + backward.astype(F32)
        forward = shift(ahead.astype(BF), 1, groups)
        backward = shift(behind.astype(BF), -1, groups)
    return terms[0].astype(F32) + forward.astype(F32) + backward.astype(F32)


def on_device(
    tokens,
    expert_ids,
    gates,
    ln_gain,
    w_in,
    b_in,
    w_out,
    b_out,
    final_gain,
    w_cross,
    lengths,
    page_table,
    queries,
):
    rows_dev, width = tokens.shape
    experts = lax.axis_size("expert")
    groups = lax.axis_size("group")
    capacity = 2 * rows_dev // experts
    places = experts * capacity
    sentences = lengths.shape[1]
    head_size = queries.shape[1]
    column = lax.axis_index("expert")
    row = lax.axis_index("group")
    first, second = w_in[0], w_out[0]

    cross_cols = w_cross.shape[1]
    shard_rows = w_cross.shape[0]
    outgoing, picks, own_cross = dispatch(tokens, expert_ids, ln_gain, w_cross, queries, places)
    cross_rows = lax.all_gather(own_cross, "group", axis=0, tiled=False)
    arrived = lax.all_to_all(outgoing, "expert", 0, 0, tiled=True).reshape(places, width)

    terms = ring_experts(arrived, lambda rows: expert_terms(rows, first, b_in, second), groups)
    cross_rows, _ = lax.optimization_barrier((cross_rows, terms[0]))
    cross_rows = side_by_side(cross_rows, shard_rows, cross_cols)
    cross = lax.all_gather(cross_rows, "expert", axis=0, tiled=True)

    sums = ring_sum(terms, groups)
    expert_out = (sums + b_out[0]).astype(BF).reshape(experts, capacity, width)
    returned = lax.all_to_all(expert_out, "expert", 0, 0, tiled=True)

    block = column * groups + row
    own_lengths = lax.dynamic_slice_in_dim(lengths, block, 1, 0)[0]
    owners = lax.dynamic_slice_in_dim(page_table, block, 1, 0)[0]
    slots_dev = groups * sentences
    ends = jnp.cumsum(own_lengths)
    query_rows = owners * slots_dev + row * sentences + jnp.arange(sentences, dtype=jnp.int32)
    info = jnp.stack([query_rows, ends - own_lengths, ends])

    encoded, own_context = tail(
        info, tokens, returned, picks, gates, final_gain, cross, groups, head_size
    )
    own_context = own_context.reshape(groups, sentences, head_size)

    slots = lax.all_to_all(own_context, "group", 0, 0, tiled=True).reshape(slots_dev, head_size)
    column_ids = jnp.arange(experts, dtype=jnp.int32)
    column_owners = lax.dynamic_slice_in_dim(page_table, column * groups, groups, 0).reshape(-1)
    to_owner = (column_ids[:, None] == column_owners[None, :]).astype(BF)
    sent = dot(to_owner, slots).astype(BF).reshape(experts, 1, head_size)
    received = lax.all_to_all(sent, "expert", 0, 0, tiled=True).reshape(experts, head_size)
    first_owners = page_table[:groups].reshape(-1)
    source = lax.rem(column - first_owners + experts, experts)
    from_source = (source[:, None] == column_ids[None, :]).astype(BF)
    context = dot(from_source, received).astype(BF)
    return (encoded, context)


def solution(mesh):
    return jax.shard_map(
        on_device,
        mesh=mesh,
        in_specs=(
            P(("expert", "group"), None),
            P(("expert", "group"), None),
            P(("expert", "group"), None),
            P(),
            P("expert", None, "group"),
            P("expert", "group"),
            P("expert", "group", None),
            P("expert", None),
            P(),
            P("expert", "group"),
            P(),
            P(),
            P("expert", "group"),
        ),
        out_specs=(P(("expert", "group"), None), P("expert", "group")),
        check_vma=False,
    )
```
